32 devices in a mesh: dp: 4 (over z), proto: 8 (over y, x, core).
Axes of the slice: x: 2, y: 2, z: 4, core: 2. Of those that a mesh axis runs over, the one named last changes fastest.
Arguments:
- embeddings: bfloat16 [8192, 2560], P('proto', 'dp'), may hold values from -26 to 26
- table: bfloat16 [32768, 2560], P('proto', 'dp'), may hold values from -5 to 5
- tile_lists: int32 [8, 8], replicated, may hold values from 0 to 255, as said below
- labels: int32 [8192], P('proto'), may hold values from 0 to 32767, as said below
Outputs:
- loss: float32 [], replicated
- grad_emb: bfloat16 [8192, 2560], P('proto', 'dp')
- grad_table: bfloat16 [32768, 2560], P('proto', 'dp')
The draws below stay inside these ranges and needn't reach their ends.
Inputs may be any that keep to these rules, and one draw needn't show every extreme that they name: `tile_lists`: each block's 8 tile ids are distinct and fall on exactly 4 owners (owner = id // 32), each of those owners holding exactly 2 of them. `labels`: the tile of each row's label (label // 128) is in the list of the row's block.
All inputs are finite; a program needn't handle non-finite values.
Results may differ from the reference program's by a relative error of at most 0.0025.
The reference program's roundings to bfloat16 on the way count: a program that leaves them out, or rounds other values in their place, can miss the bound.
Values may be sent and summed in bfloat16 or wider, within the bound.
A program may use at most 128 MiB of HBM per device.

```python
import math
import jax
import jax.numpy as jnp
from jax import lax

D = 2560
TILE = 128
CAP = 2
TILES_DEV = 32
K = 8
BLOCK = 1024
BLOCKS = 8
ROWS = 8192
NPROTO = 32768


def make_lists(key):
    base = jax.random.fold_in(key, 101)
    keys = jax.random.split(base, BLOCKS)

    def one_block(block_key):
        first_key, second_key = jax.random.split(block_key)
        owners = jax.random.permutation(first_key, BLOCKS)[:K // CAP]
        picks = jax.vmap(lambda inner: jax.random.permutation(inner, TILES_DEV)[:CAP])(jax.random.split(second_key, K // CAP))
        return (owners[:, None] * TILES_DEV + picks).reshape(K).astype(jnp.int32)
    return jax.vmap(one_block)(keys)


def make_labels(key):
    lists = make_lists(key)
    first_key, second_key = jax.random.split(jax.random.fold_in(key, 202))
    slot = jax.random.randint(first_key, (BLOCKS, BLOCK), 0, K)
    offset = jax.random.randint(second_key, (BLOCKS, BLOCK), 0, TILE)
    chosen = jnp.take_along_axis(lists, slot, axis=1)
    return (chosen * TILE + offset).reshape(ROWS).astype(jnp.int32)


def table_rows(key, index):
    base = jax.random.fold_in(key, 303)

    def one_row(row):
        row_key = jax.random.fold_in(base, row)
        return jnp.clip(jax.random.normal(row_key, (D,), jnp.float32), -5.0, 5.0)
    return jax.vmap(one_row)(index)


def draw_tile_lists(key, part):
    return make_lists(key)


def draw_labels(key, part):
    return make_labels(key)


def draw_table(key, part):
    return table_rows(key, jnp.arange(NPROTO, dtype=jnp.int32)).astype(jnp.bfloat16)


def draw_embeddings(key, part):
    base = jax.random.fold_in(key, 404)
    return jnp.clip(jax.random.normal(base, (ROWS, D), jnp.float32), -5.0, 5.0).astype(jnp.bfloat16)


def setup_inputs(seed: int = 0) -> dict:
    key_of = jax.random.split(jax.random.key(seed), 5)
    return {
        "embeddings": draw_embeddings(jax.random.fold_in(key_of[4], 71), 0),
        "table": draw_table(jax.random.fold_in(key_of[4], 71), 0),
        "tile_lists": draw_tile_lists(jax.random.fold_in(key_of[4], 71), 0),
        "labels": draw_labels(jax.random.fold_in(key_of[4], 71), 0),
    }


def block_terms(emb_block, table, ids, lab):
    tiles = jnp.take(table.reshape(TILES_DEV * BLOCKS, TILE, D), ids, axis=0).reshape(K * TILE, D)
    scores = lax.dot_general(emb_block, tiles, (((1,), (1,)), ((), ())), preferred_element_type=jnp.float32) / math.sqrt(D)
    hit = (ids[None, :] == (lab // TILE)[:, None]).astype(jnp.int32)
    column = lax.optimization_barrier(jnp.sum(hit * (jnp.arange(K, dtype=jnp.int32) * TILE)[None, :], axis=1)) + lab % TILE
    onehot = (jnp.arange(K * TILE, dtype=jnp.int32)[None, :] == column[:, None]).astype(jnp.float32)
    top = lax.optimization_barrier(jnp.max(scores, axis=1, keepdims=True))
    expo = jnp.exp(scores - top)
    total = lax.optimization_barrier(jnp.sum(expo, axis=1, keepdims=True))
    lse = top[:, 0] + jnp.log(total[:, 0])
    target = lax.optimization_barrier(jnp.sum(scores * onehot, axis=1))
    loss_sum = jnp.sum(lse - target)
    dz_block = (expo / total - onehot).astype(jnp.bfloat16)
    grad_rows = jnp.dot(dz_block, tiles, preferred_element_type=jnp.float32).astype(jnp.bfloat16)
    piece = lax.dot_general(dz_block, emb_block, (((0,), (0,)), ((), ())), preferred_element_type=jnp.float32).astype(jnp.bfloat16)
    return (loss_sum, grad_rows, piece)

def reference(embeddings, table, tile_lists, labels):
    emb_blocks = embeddings.reshape(BLOCKS, BLOCK, D)
    lab_blocks = labels.reshape(BLOCKS, BLOCK)

    def step(carry, inputs):
        accum, loss_acc = carry
        emb_block, ids, lab = inputs
        loss_sum, grad_rows, piece = block_terms(emb_block, table, ids, lab)
        accum = accum.at[ids].add(piece.reshape(K, TILE, D).astype(jnp.float32))
        return ((accum, loss_acc + loss_sum), grad_rows)
    start = (jnp.zeros((TILES_DEV * BLOCKS, TILE, D), jnp.float32), jnp.zeros((), jnp.float32))
    (accum, loss_acc), grads = lax.scan(step, start, (emb_blocks, tile_lists, lab_blocks))
    loss = loss_acc / ROWS
    grad_emb = grads.reshape(ROWS, D)
    grad_table = accum.reshape(NPROTO, D).astype(jnp.bfloat16)
    return (loss, grad_emb, grad_table)
```

```python
import functools
import math

import jax
import jax.numpy as jnp
from jax import lax
from jax.experimental import pallas as pl
from jax.experimental.pallas import tpu as pltpu
from jax.sharding import PartitionSpec as P

D = 2560
TILE = 128
CAP = 2
CHUNK = 16
LAG = 3
VMEM_LIMIT = 56 * 2**20
MESH = pl.DeviceIdType.MESH


def slot_plan(ids, tiles_here):
    owners = ids // tiles_here
    local = ids % tiles_here
    count = ids.shape[-1]
    before = jnp.arange(count)[:, None] > jnp.arange(count)[None, :]
    earlier = (owners[..., :, None] == owners[..., None, :]) & before
    rank = jnp.sum(earlier.astype(jnp.int32), axis=-1)
    return (owners, local, rank)


def softmax_terms(scores, ids, lab, list_len):
    hit = (ids[None, :] == (lab // TILE)[:, None]).astype(jnp.int32)
    column = (
        jnp.sum(hit * (jnp.arange(list_len, dtype=jnp.int32) * TILE)[None, :], axis=1) + lab % TILE
    )
    onehot = (jnp.arange(list_len * TILE, dtype=jnp.int32)[None, :] == column[:, None]).astype(
        jnp.float32
    )
    top = jnp.max(scores, axis=1, keepdims=True)
    expo = jnp.exp(scores - top)
    total = jnp.sum(expo, axis=1, keepdims=True)
    lse = top[:, 0] + jnp.log(total[:, 0])
    target = jnp.sum(scores * onehot, axis=1)
    dz_rows = (expo / total - onehot).astype(jnp.bfloat16)
    return (jnp.sum(lse - target), dz_rows)


def body(embeddings, table, tile_lists, labels):
    block_rows, width = embeddings.shape
    list_len = tile_lists.shape[1]
    tiles_here = table.shape[0] // TILE
    groups = lax.axis_size("proto")
    dp_count = lax.axis_size("dp")
    rows_dev = block_rows // dp_count
    total_rows = block_rows * groups
    me = lax.axis_index("proto")
    part = lax.axis_index("dp")
    inv_scale = 1.0 / math.sqrt(D)
    owners, local, rank = slot_plan(tile_lists, tiles_here)
    match = (owners == me)[:, :, None] & (
        rank[:, :, None] == jnp.arange(CAP, dtype=jnp.int32)[None, None, :]
    )
    select = jnp.sum(match.astype(jnp.int32) * local[:, :, None], axis=1)
    shaped_table = table.reshape(tiles_here, TILE, width)
    outgoing = pack_tiles(shaped_table, select.reshape(-1)).reshape(groups, CAP, TILE, width)
    incoming = lax.all_to_all(outgoing, "proto", split_axis=0, concat_axis=0, tiled=True)
    my_ids = lax.dynamic_index_in_dim(tile_lists, me, 0, keepdims=False)
    my_owner = lax.dynamic_index_in_dim(owners, me, 0, keepdims=False)
    my_rank = lax.dynamic_index_in_dim(rank, me, 0, keepdims=False)
    flat_slot = my_owner * CAP + my_rank
    tiles = pack_tiles(incoming.reshape(groups * CAP, TILE, width), flat_slot).reshape(
        list_len * TILE, width
    )
    scores = (
        lax.psum_scatter(
            lax.dot_general(
                embeddings, tiles, (((1,), (1,)), ((), ())), preferred_element_type=jnp.float32
            ),
            "dp",
            scatter_dimension=0,
            tiled=True,
        )
        * inv_scale
    )
    my_labels = lax.dynamic_slice_in_dim(labels, part * rows_dev, rows_dev, 0)
    loss_part, dz_rows = softmax_terms(scores, my_ids, my_labels, list_len)
    dz_block = lax.all_gather(dz_rows, "dp", axis=0, tiled=True)
    loss = lax.psum(loss_part, ("dp", "proto")) / total_rows
    grad_emb = jnp.dot(dz_block, tiles, preferred_element_type=jnp.float32).astype(jnp.bfloat16)
    piece = lax.dot_general(
        dz_block, embeddings, (((0,), (0,)), ((), ())), preferred_element_type=jnp.float32
    ).astype(jnp.bfloat16)
    returning = (
        jnp.zeros((groups * CAP, TILE, width), jnp.bfloat16)
        .at[flat_slot]
        .set(piece.reshape(list_len, TILE, width))
    )
    returned = lax.all_to_all(
        returning.reshape(groups, CAP, TILE, width),
        "proto",
        split_axis=0,
        concat_axis=0,
        tiled=True,
    )
    accum = (
        jnp.zeros((tiles_here, TILE, width), jnp.float32)
        .at[select.reshape(-1)]
        .add(returned.reshape(groups * CAP, TILE, width))
    )
    grad_table = accum.reshape(tiles_here * TILE, width).astype(jnp.bfloat16)
    return (loss, grad_emb, grad_table)


def pack_kernel(pick_ref, table_ref, out_ref, sems):
    count = out_ref.shape[0]

    def copy(slot):
        return pltpu.make_async_copy(
            table_ref.at[pick_ref[slot]], out_ref.at[slot], sems.at[slot]
        )

    for slot in range(count):
        copy(slot).start()
    for slot in range(count):
        copy(slot).wait()


def pack_tiles(shaped_table, pick):
    count = pick.shape[0]
    _, tile, width = shaped_table.shape
    return pl.pallas_call(
        pack_kernel,
        out_shape=jax.ShapeDtypeStruct((count, tile, width), shaped_table.dtype),
        grid_spec=pltpu.PrefetchScalarGridSpec(
            num_scalar_prefetch=1,
            grid=(1,),
            in_specs=[pl.BlockSpec(memory_space=pl.ANY)],
            out_specs=pl.BlockSpec(memory_space=pl.ANY),
            scratch_shapes=[pltpu.SemaphoreType.DMA((count,))],
        ),
    )(pick, shaped_table)


def place_kernel(per_step, count, pick_ref, got_ref, out_ref, acc_ref):
    step = pl.program_id(0)
    for inner in range(per_step):
        tile_id = step * per_step + inner
        acc_ref[...] = jnp.zeros_like(acc_ref)

        def add(slot, carry):
            @pl.when(pick_ref[slot] == tile_id)
            def _():
                acc_ref[...] += got_ref[slot].astype(jnp.float32)

            return carry

        lax.fori_loop(0, count, add, 0)
        out_ref[inner] = acc_ref[...].astype(out_ref.dtype)


def place_tiles(returned, pick, tiles_here):
    count, tile, width = returned.shape
    per_step = 4
    return pl.pallas_call(
        functools.partial(place_kernel, per_step, count),
        out_shape=jax.ShapeDtypeStruct((tiles_here, tile, width), returned.dtype),
        grid_spec=pltpu.PrefetchScalarGridSpec(
            num_scalar_prefetch=1,
            grid=(tiles_here // per_step,),
            in_specs=[pl.BlockSpec(memory_space=pltpu.VMEM)],
            out_specs=pl.BlockSpec((per_step, tile, width), lambda i, pick: (i, 0, 0)),
            scratch_shapes=[pltpu.VMEM((tile, width), jnp.float32)],
        ),
        compiler_params=pltpu.CompilerParams(vmem_limit_bytes=24 * 2**20),
    )(pick, returned)


def main_kernel(
    groups,
    dp_count,
    inv_scale,
    slot_ref,
    back_ref,
    out_tiles,
    emb,
    column,
    grad_emb,
    returned,
    loss_out,
    incoming,
    tiles,
    scores,
    partial,
    dz,
    piece,
    ret,
    loss_acc,
    loss_mine,
    loss_plane,
    loss_sum,
    loss_z,
    tile_send,
    tile_recv,
    own_sem,
    part_send,
    part_recv,
    dz_send,
    dz_recv,
    ret_send,
    ret_recv,
    own_ret_sem,
    lp_send,
    lp_recv,
    lz_send,
    lz_recv,
):
    me = lax.axis_index("proto")
    z = lax.axis_index("dp")
    rows, width = emb.shape
    list_len = slot_ref.shape[0]
    cols = list_len * TILE
    half = rows // 2
    chunks = half // CHUNK
    last = dp_count - 1

    barrier = pltpu.get_barrier_semaphore()
    for k in range(1, groups):
        pl.semaphore_signal(
            barrier, inc=1, device_id={"proto": lax.rem(me + k, groups)}, device_id_type=MESH
        )
    for k in range(1, dp_count):
        pl.semaphore_signal(
            barrier, inc=1, device_id={"dp": lax.rem(z + k, dp_count)}, device_id_type=MESH
        )
    pl.semaphore_wait(barrier, groups + dp_count - 2)

    def tile_copy(k):
        to = lax.rem(me + k, groups)
        return pltpu.make_async_remote_copy(
            src_ref=out_tiles.at[pl.ds(to * CAP, CAP)],
            dst_ref=incoming.at[pl.ds(me * CAP, CAP)],
            send_sem=tile_send.at[k],
            recv_sem=tile_recv.at[k],
            device_id={"proto": to},
            device_id_type=MESH,
        )

    for k in range(1, groups):
        tile_copy(k).start()
    own = pltpu.make_async_copy(
        out_tiles.at[pl.ds(me * CAP, CAP)], incoming.at[pl.ds(me * CAP, CAP)], own_sem
    )
    own.start()
    loss_acc[...] = jnp.zeros_like(loss_acc)
    own.wait()
    for k in range(1, groups):
        tile_copy(k).wait()
    for j in range(list_len):
        tiles[j * TILE : (j + 1) * TILE, :] = incoming[slot_ref[j]]

    block = min(256, half)

    def score_block(i, carry):
        at = pl.ds(pl.multiple_of(i * block, block), block)
        scores[at, :] = lax.dot_general(
            emb[at, :], tiles[...], (((1,), (1,)), ((), ())), preferred_element_type=jnp.float32
        )
        return carry

    lax.fori_loop(0, rows // block, score_block, 0)

    def rows_of(way, c):
        return pl.multiple_of((1 - way) * half + c * CHUNK, CHUNK)

    def part_copy(way, c, first):
        dst = partial.at[way, pl.ds(pl.multiple_of(c * CHUNK, CHUNK), CHUNK)]
        src = scores.at[pl.ds(rows_of(way, c), CHUNK)] if first else dst
        return pltpu.make_async_remote_copy(
            src_ref=src,
            dst_ref=dst,
            send_sem=part_send.at[way, c],
            recv_sem=part_recv.at[way, c],
            device_id={"dp": jnp.clip(z + 1 - 2 * way, 0, last)},
            device_id_type=MESH,
        )

    def dz_copy(way, c):
        at = dz.at[pl.ds(rows_of(way, c), CHUNK)]
        return pltpu.make_async_remote_copy(
            src_ref=at,
            dst_ref=at,
            send_sem=dz_send.at[way, c],
            recv_sem=dz_recv.at[way, c],
            device_id={"dp": jnp.clip(z - 1 + 2 * way, 0, last)},
            device_id_type=MESH,
        )

    lane = lax.broadcasted_iota(jnp.int32, (CHUNK, cols), 1)

    def step(i, carry):
        way = lax.rem(i, 2)
        s = i // 2
        pos = jnp.where(way == 0, z, last - z)
        c = s - LAG * pos

        @pl.when((c >= 0) & (c < chunks))
        def _():
            at = pl.ds(rows_of(way, c), CHUNK)
            here = pl.ds(pl.multiple_of(c * CHUNK, CHUNK), CHUNK)

            @pl.when(pos == 0)
            def _():
                part_copy(way, c, True).start()

            @pl.when((pos > 0) & (pos < last))
            def _():
                part_copy(way, c, False).wait_recv()
                partial[way, here, :] += scores[at, :]
                part_copy(way, c, False).start()

            @pl.when(pos == last)
            def _():
                part_copy(way, c, False).wait_recv()
                score = (partial[way, here, :] + scores[at, :]) * inv_scale
                onehot = lane == column[at, :]
                top = jnp.max(score, axis=1, keepdims=True)
                expo = jnp.exp(score - top)
                total = jnp.sum(expo, axis=1, keepdims=True)
                target = jnp.sum(jnp.where(onehot, score, 0.0), axis=1, keepdims=True)
                loss_acc[...] += (top + jnp.log(total)) - target + jnp.zeros_like(loss_acc)
                dz[at, :] = (expo / total - jnp.where(onehot, 1.0, 0.0)).astype(dz.dtype)
                dz_copy(way, c).start()

        c2 = s - LAG * last - LAG * (last - pos)

        @pl.when((c2 >= 0) & (c2 < chunks) & (pos < last))
        def _():
            dz_copy(way, c2).wait_recv()

            @pl.when(pos > 0)
            def _():
                dz_copy(way, c2).start()

        return carry

    lax.fori_loop(0, 2 * (chunks + 2 * LAG * last), step, 0)

    loss_mine[...] = jnp.broadcast_to(jnp.sum(loss_acc[...], axis=0, keepdims=True), (8, 128))

    def lp_copy(k):
        return pltpu.make_async_remote_copy(
            src_ref=loss_mine,
            dst_ref=loss_plane.at[me],
            send_sem=lp_send.at[k],
            recv_sem=lp_recv.at[k],
            device_id={"proto": lax.rem(me + k, groups)},
            device_id_type=MESH,
        )

    for k in range(1, groups):
        lp_copy(k).start()

    wide = min(256, cols)
    for j in range(cols // wide):
        out = lax.dot_general(
            dz[:, j * wide : (j + 1) * wide],
            emb[...],
            (((0,), (0,)), ((), ())),
            preferred_element_type=jnp.float32,
        ).astype(piece.dtype)
        for t in range(wide // TILE):
            piece[j * (wide // TILE) + t] = out[t * TILE : (t + 1) * TILE, :]

    def ret_copy(k):
        to = lax.rem(me + k, groups)
        return pltpu.make_async_remote_copy(
            src_ref=ret.at[pl.ds(to * CAP, CAP)],
            dst_ref=returned.at[pl.ds(me * CAP, CAP)],
            send_sem=ret_send.at[k],
            recv_sem=ret_recv.at[k],
            device_id={"proto": to},
            device_id_type=MESH,
        )

    for k in range(1, groups):
        to = lax.rem(me + k, groups)
        for t in range(CAP):
            ret[to * CAP + t] = piece[back_ref[to * CAP + t]]
        ret_copy(k).start()
    for t in range(CAP):
        ret[me * CAP + t] = piece[back_ref[me * CAP + t]]
    own_ret = pltpu.make_async_copy(
        ret.at[pl.ds(me * CAP, CAP)], returned.at[pl.ds(me * CAP, CAP)], own_ret_sem
    )
    own_ret.start()

    def grad_block(i, carry):
        at = pl.ds(pl.multiple_of(i * block, block), block)
        grad_emb[at, :] = jnp.dot(
            dz[at, :], tiles[...], preferred_element_type=jnp.float32
        ).astype(grad_emb.dtype)
        return carry

    lax.fori_loop(0, rows // block, grad_block, 0)

    loss_plane[me] = loss_mine[...]
    for k in range(1, groups):
        lp_copy(k).wait()
    plane = loss_plane[0]
    for k in range(1, groups):
        plane = plane + loss_plane[k]
    loss_sum[...] = plane

    def lz_copy(k):
        return pltpu.make_async_remote_copy(
            src_ref=loss_sum,
            dst_ref=loss_z.at[z],
            send_sem=lz_send.at[k],
            recv_sem=lz_recv.at[k],
            device_id={"dp": lax.rem(z + k, dp_count)},
            device_id_type=MESH,
        )

    for k in range(1, dp_count):
        lz_copy(k).start()
    loss_z[z] = plane
    for k in range(1, dp_count):
        lz_copy(k).wait()
    whole = loss_z[0]
    for k in range(1, dp_count):
        whole = whole + loss_z[k]
    loss_out[...] = whole

    def drain(i, carry):
        way = lax.rem(i, 2)
        c = i // 2
        pos = jnp.where(way == 0, z, last - z)

        @pl.when(pos < last)
        def _():
            part_copy(way, c, False).wait_send()

        @pl.when(pos > 0)
        def _():
            dz_copy(way, c).wait_send()

        return carry

    lax.fori_loop(0, 2 * chunks, drain, 0)
    own_ret.wait()
    for k in range(1, groups):
        ret_copy(k).wait()


def fused_body(embeddings, table, tile_lists, labels):
    block_rows, width = embeddings.shape
    list_len = tile_lists.shape[1]
    tiles_here = table.shape[0] // TILE
    groups = lax.axis_size("proto")
    dp_count = lax.axis_size("dp")
    total_rows = block_rows * groups
    cols = list_len * TILE
    slots = groups * CAP
    me = lax.axis_index("proto")
    owners, local, rank = slot_plan(tile_lists, tiles_here)
    match = (owners == me)[:, :, None] & (
        rank[:, :, None] == jnp.arange(CAP, dtype=jnp.int32)[None, None, :]
    )
    select = jnp.sum(match.astype(jnp.int32) * local[:, :, None], axis=1).reshape(-1)
    taken = jnp.any(match, axis=1).reshape(-1)
    my_ids = lax.dynamic_index_in_dim(tile_lists, me, 0, keepdims=False)
    flat = owners * CAP + rank
    my_slot = lax.dynamic_index_in_dim(flat, me, 0, keepdims=False)
    order = jnp.arange(list_len, dtype=jnp.int32)
    back = jnp.sum(
        (my_slot[None, :] == jnp.arange(slots, dtype=jnp.int32)[:, None]).astype(jnp.int32)
        * order[None, :],
        axis=1,
    )
    hit = (my_ids[None, :] == (labels // TILE)[:, None]).astype(jnp.int32)
    column = (jnp.sum(hit * (order * TILE)[None, :], axis=1) + labels % TILE)[:, None]
    outgoing = pack_tiles(table.reshape(tiles_here, TILE, width), select)
    chunks = block_rows // 2 // CHUNK
    bf16, f32 = jnp.bfloat16, jnp.float32
    dma = pltpu.SemaphoreType.DMA
    vmem = pl.BlockSpec(memory_space=pltpu.VMEM)
    smem = pl.BlockSpec(memory_space=pltpu.SMEM)
    hbm = pl.BlockSpec(memory_space=pl.ANY)
    grad_emb, returned, loss = pl.pallas_call(
        functools.partial(main_kernel, groups, dp_count, 1.0 / math.sqrt(D)),
        out_shape=(
            jax.ShapeDtypeStruct((block_rows, width), bf16),
            jax.ShapeDtypeStruct((slots, TILE, width), bf16),
            jax.ShapeDtypeStruct((8, 128), f32),
        ),
        in_specs=[smem, smem, hbm, vmem, vmem],
        out_specs=(vmem, hbm, vmem),
        scratch_shapes=[
            pltpu.VMEM((slots, TILE, width), bf16),
            pltpu.VMEM((cols, width), bf16),
            pltpu.VMEM((block_rows, cols), f32),
            pltpu.VMEM((2, block_rows // 2, cols), f32),
            pltpu.VMEM((block_rows, cols), bf16),
            pltpu.VMEM((list_len, TILE, width), bf16),
            pltpu.VMEM((slots, TILE, width), bf16),
            pltpu.VMEM((CHUNK, 128), f32),
            pltpu.VMEM((8, 128), f32),
            pltpu.VMEM((groups, 8, 128), f32),
            pltpu.VMEM((8, 128), f32),
            pltpu.VMEM((dp_count, 8, 128), f32),
            dma((groups,)),
            dma((groups,)),
            dma,
            dma((2, chunks)),
            dma((2, chunks)),
            dma((2, chunks)),
            dma((2, chunks)),
            dma((groups,)),
            dma((groups,)),
            dma,
            dma((groups,)),
            dma((groups,)),
            dma((dp_count,)),
            dma((dp_count,)),
        ],
        compiler_params=pltpu.CompilerParams(
            collective_id=0, has_side_effects=True, vmem_limit_bytes=VMEM_LIMIT
        ),
    )(my_slot, back, outgoing, embeddings, column)
    grad_table = place_tiles(returned, jnp.where(taken, select, -1), tiles_here)
    return (loss[0, 0] / total_rows, grad_emb, grad_table.reshape(tiles_here * TILE, width))


def fused_bytes(block_rows, width, list_len, groups):
    cols = list_len * TILE
    slots = groups * CAP
    return (
        block_rows * cols * (4 + 4 + 2)
        + 2 * slots * TILE * width * 2
        + 2 * cols * width * 2
        + 2 * block_rows * width * 2
        + block_rows * 128 * 4
    )


def any_body(embeddings, table, tile_lists, labels):
    need = fused_bytes(*embeddings.shape, tile_lists.shape[1], lax.axis_size("proto"))
    if need + 12 * 2**20 <= VMEM_LIMIT:
        return fused_body(embeddings, table, tile_lists, labels)
    return body(embeddings, table, tile_lists, labels)


def solution(mesh):
    placed = (P("proto", "dp"), P("proto", "dp"), P(), P("proto"))
    return jax.shard_map(
        any_body,
        mesh=mesh,
        in_specs=placed,
        out_specs=(P(), P("proto", "dp"), P("proto", "dp")),
        check_vma=False,
    )
```

```python
import functools
import math

import jax
import jax.numpy as jnp
from jax import lax
from jax.experimental import pallas as pl
from jax.experimental.pallas import tpu as pltpu
from jax.sharding import PartitionSpec as P

D = 2560
TILE = 128
CAP = 2
CHUNK = 16
LAG = 3
VMEM_LIMIT = 56 * 2**20
MESH = pl.DeviceIdType.MESH


def slot_plan(ids, tiles_here):
    owners = ids // tiles_here
    local = ids % tiles_here
    count = ids.shape[-1]
    before = jnp.arange(count)[:, None] > jnp.arange(count)[None, :]
    earlier = (owners[..., :, None] == owners[..., None, :]) & before
    rank = jnp.sum(earlier.astype(jnp.int32), axis=-1)
    return (owners, local, rank)


def softmax_terms(scores, ids, lab, list_len):
    hit = (ids[None, :] == (lab // TILE)[:, None]).astype(jnp.int32)
    column = (
        jnp.sum(hit * (jnp.arange(list_len, dtype=jnp.int32) * TILE)[None, :], axis=1) + lab % TILE
    )
    onehot = (jnp.arange(list_len * TILE, dtype=jnp.int32)[None, :] == column[:, None]).astype(
        jnp.float32
    )
    top = jnp.max(scores, axis=1, keepdims=True)
    expo = jnp.exp(scores - top)
    total = jnp.sum(expo, axis=1, keepdims=True)
    lse = top[:, 0] + jnp.log(total[:, 0])
    target = jnp.sum(scores * onehot, axis=1)
    dz_rows = (expo / total - onehot).astype(jnp.bfloat16)
    return (jnp.sum(lse - target), dz_rows)


def body(embeddings, table, tile_lists, labels):
    block_rows, width = embeddings.shape
    list_len = tile_lists.shape[1]
    tiles_here = table.shape[0] // TILE
    groups = lax.axis_size("proto")
    dp_count = lax.axis_size("dp")
    rows_dev = block_rows // dp_count
    total_rows = block_rows * groups
    me = lax.axis_index("proto")
    part = lax.axis_index("dp")
    inv_scale = 1.0 / math.sqrt(D)
    owners, local, rank = slot_plan(tile_lists, tiles_here)
    match = (owners == me)[:, :, None] & (
        rank[:, :, None] == jnp.arange(CAP, dtype=jnp.int32)[None, None, :]
    )
    select = jnp.sum(match.astype(jnp.int32) * local[:, :, None], axis=1)
    shaped_table = table.reshape(tiles_here, TILE, width)
    outgoing = pack_tiles(shaped_table, select.reshape(-1)).reshape(groups, CAP, TILE, width)
    incoming = lax.all_to_all(outgoing, "proto", split_axis=0, concat_axis=0, tiled=True)
    my_ids = lax.dynamic_index_in_dim(tile_lists, me, 0, keepdims=False)
    my_owner = lax.dynamic_index_in_dim(owners, me, 0, keepdims=False)
    my_rank = lax.dynamic_index_in_dim(rank, me, 0, keepdims=False)
    flat_slot = my_owner * CAP + my_rank
    tiles = pack_tiles(incoming.reshape(groups * CAP, TILE, width), flat_slot).reshape(
        list_len * TILE, width
    )
    scores = (
        lax.psum_scatter(
            lax.dot_general(
                embeddings, tiles, (((1,), (1,)), ((), ())), preferred_element_type=jnp.float32
            ),
            "dp",
            scatter_dimension=0,
            tiled=True,
        )
        * inv_scale
    )
    my_labels = lax.dynamic_slice_in_dim(labels, part * rows_dev, rows_dev, 0)
    loss_part, dz_rows = softmax_terms(scores, my_ids, my_labels, list_len)
    dz_block = lax.all_gather(dz_rows, "dp", axis=0, tiled=True)
    loss = lax.psum(loss_part, ("dp", "proto")) / total_rows
    grad_emb = jnp.dot(dz_block, tiles, preferred_element_type=jnp.float32).astype(jnp.bfloat16)
    piece = lax.dot_general(
        dz_block, embeddings, (((0,), (0,)), ((), ())), preferred_element_type=jnp.float32
    ).astype(jnp.bfloat16)
    returning = (
        jnp.zeros((groups * CAP, TILE, width), jnp.bfloat16)
        .at[flat_slot]
        .set(piece.reshape(list_len, TILE, width))
    )
    returned = lax.all_to_all(
        returning.reshape(groups, CAP, TILE, width),
        "proto",
        split_axis=0,
        concat_axis=0,
        tiled=True,
    )
    accum = (
        jnp.zeros((tiles_here, TILE, width), jnp.float32)
        .at[select.reshape(-1)]
        .add(returned.reshape(groups * CAP, TILE, width))
    )
    grad_table = accum.reshape(tiles_here * TILE, width).astype(jnp.bfloat16)
    return (loss, grad_emb, grad_table)


def pack_kernel(pick_ref, table_ref, out_ref, sems):
    count = out_ref.shape[0]

    def copy(slot):
        return pltpu.make_async_copy(
            table_ref.at[pick_ref[slot]], out_ref.at[slot], sems.at[slot]
        )

    for slot in range(count):
        copy(slot).start()
    for slot in range(count):
        copy(slot).wait()


def pack_tiles(shaped_table, pick):
    count = pick.shape[0]
    _, tile, width = shaped_table.shape
    return pl.pallas_call(
        pack_kernel,
        out_shape=jax.ShapeDtypeStruct((count, tile, width), shaped_table.dtype),
        grid_spec=pltpu.PrefetchScalarGridSpec(
            num_scalar_prefetch=1,
            grid=(1,),
            in_specs=[pl.BlockSpec(memory_space=pl.ANY)],
            out_specs=pl.BlockSpec(memory_space=pltpu.VMEM),
            scratch_shapes=[pltpu.SemaphoreType.DMA((count,))],
        ),
        compiler_params=pltpu.CompilerParams(vmem_limit_bytes=32 * 2**20),
    )(pick, shaped_table)


def place_kernel(per_step, count, pick_ref, uses_ref, first_ref, got_ref, out_ref, acc_ref):
    step = pl.program_id(0)
    for inner in range(per_step):
        tile_id = step * per_step + inner
        uses = uses_ref[tile_id]

        @pl.when(uses == 0)
        def _():
            out_ref[inner] = jnp.zeros(out_ref.shape[1:], out_ref.dtype)

        @pl.when(uses == 1)
        def _():
            out_ref[inner] = got_ref[first_ref[tile_id]]

        @pl.when(uses > 1)
        def _():
            acc_ref[...] = jnp.zeros_like(acc_ref)

            def add(slot, carry):
                @pl.when(pick_ref[slot] == tile_id)
                def _():
                    acc_ref[...] += got_ref[slot].astype(jnp.float32)

                return carry

            lax.fori_loop(0, count, add, 0)
            out_ref[inner] = acc_ref[...].astype(out_ref.dtype)


def place_tiles(returned, pick, tiles_here):
    count, tile, width = returned.shape
    per_step = 4
    named = pick[None, :] == jnp.arange(tiles_here, dtype=jnp.int32)[:, None]
    uses = jnp.sum(named.astype(jnp.int32), axis=1)
    first = jnp.max(named * jnp.arange(count, dtype=jnp.int32)[None, :], axis=1)
    return pl.pallas_call(
        functools.partial(place_kernel, per_step, count),
        out_shape=jax.ShapeDtypeStruct((tiles_here, tile, width), returned.dtype),
        grid_spec=pltpu.PrefetchScalarGridSpec(
            num_scalar_prefetch=3,
            grid=(tiles_here // per_step,),
            in_specs=[pl.BlockSpec(memory_space=pltpu.VMEM)],
            out_specs=pl.BlockSpec((per_step, tile, width), lambda i, *refs: (i, 0, 0)),
            scratch_shapes=[pltpu.VMEM((tile, width), jnp.float32)],
        ),
        compiler_params=pltpu.CompilerParams(vmem_limit_bytes=24 * 2**20),
    )(pick, uses, first, returned)


def main_kernel(
    groups,
    dp_count,
    inv_scale,
    slot_ref,
    back_ref,
    out_tiles,
    emb,
    column,
    grad_emb,
    returned,
    loss_out,
    incoming,
    tiles,
    scores,
    partial,
    dz,
    piece,
    ret,
    loss_acc,
    loss_mine,
    loss_plane,
    loss_sum,
    loss_z,
    tile_send,
    tile_recv,
    own_sem,
    part_send,
    part_recv,
    dz_send,
    dz_recv,
    ret_send,
    ret_recv,
    own_ret_sem,
    lp_send,
    lp_recv,
    lz_send,
    lz_recv,
):
    me = lax.axis_index("proto")
    z = lax.axis_index("dp")
    rows, width = emb.shape
    list_len = slot_ref.shape[0]
    cols = list_len * TILE
    half = rows // 2
    chunks = half // CHUNK
    last = dp_count - 1

    barrier = pltpu.get_barrier_semaphore()
    for k in range(1, groups):
        pl.semaphore_signal(
            barrier, inc=1, device_id={"proto": lax.rem(me + k, groups)}, device_id_type=MESH
        )
    for k in range(1, dp_count):
        pl.semaphore_signal(
            barrier, inc=1, device_id={"dp": lax.rem(z + k, dp_count)}, device_id_type=MESH
        )
    pl.semaphore_wait(barrier, groups + dp_count - 2)

    def tile_copy(k):
        to = lax.rem(me + k, groups)
        return pltpu.make_async_remote_copy(
            src_ref=out_tiles.at[pl.ds(to * CAP, CAP)],
            dst_ref=incoming.at[pl.ds(me * CAP, CAP)],
            send_sem=tile_send.at[k],
            recv_sem=tile_recv.at[k],
            device_id={"proto": to},
            device_id_type=MESH,
        )

    for k in range(1, groups):
        tile_copy(k).start()
    own = pltpu.make_async_copy(
        out_tiles.at[pl.ds(me * CAP, CAP)], incoming.at[pl.ds(me * CAP, CAP)], own_sem
    )
    own.start()
    loss_acc[...] = jnp.zeros_like(loss_acc)
    own.wait()
    for k in range(1, groups):
        tile_copy(k).wait()
    for j in range(list_len):
        tiles[j * TILE : (j + 1) * TILE, :] = incoming[slot_ref[j]]

    block = min(256, half)

    def score_block(i, carry):
        at = pl.ds(pl.multiple_of(i * block, block), block)
        scores[at, :] = lax.dot_general(
            emb[at, :], tiles[...], (((1,), (1,)), ((), ())), preferred_element_type=jnp.float32
        )
        return carry

    lax.fori_loop(0, rows // block, score_block, 0)

    def rows_of(way, c):
        return pl.multiple_of((1 - way) * half + c * CHUNK, CHUNK)

    def part_copy(way, c, first):
        dst = partial.at[way, pl.ds(pl.multiple_of(c * CHUNK, CHUNK), CHUNK)]
        src = scores.at[pl.ds(rows_of(way, c), CHUNK)] if first else dst
        return pltpu.make_async_remote_copy(
            src_ref=src,
            dst_ref=dst,
            send_sem=part_send.at[way, c],
            recv_sem=part_recv.at[way, c],
            device_id={"dp": jnp.clip(z + 1 - 2 * way, 0, last)},
            device_id_type=MESH,
        )

    def dz_copy(way, c):
        at = dz.at[pl.ds(rows_of(way, c), CHUNK)]
        return pltpu.make_async_remote_copy(
            src_ref=at,
            dst_ref=at,
            send_sem=dz_send.at[way, c],
            recv_sem=dz_recv.at[way, c],
            device_id={"dp": jnp.clip(z - 1 + 2 * way, 0, last)},
            device_id_type=MESH,
        )

    lane = lax.broadcasted_iota(jnp.int32, (CHUNK, cols), 1)

    def step(i, carry):
        way = lax.rem(i, 2)
        s = i // 2
        pos = jnp.where(way == 0, z, last - z)
        c = s - LAG * pos

        @pl.when((c >= 0) & (c < chunks))
        def _():
            at = pl.ds(rows_of(way, c), CHUNK)
            here = pl.ds(pl.multiple_of(c * CHUNK, CHUNK), CHUNK)

            @pl.when(pos == 0)
            def _():
                part_copy(way, c, True).start()

            @pl.when((pos > 0) & (pos < last))
            def _():
                part_copy(way, c, False).wait_recv()
                partial[way, here, :] += scores[at, :]
                part_copy(way, c, False).start()

            @pl.when(pos == last)
            def _():
                part_copy(way, c, False).wait_recv()
                score = (partial[way, here, :] + scores[at, :]) * inv_scale
                onehot = lane == column[at, :]
                top = jnp.max(score, axis=1, keepdims=True)
                expo = jnp.exp(score - top)
                total = jnp.sum(expo, axis=1, keepdims=True)
                target = jnp.sum(jnp.where(onehot, score, 0.0), axis=1, keepdims=True)
                loss_acc[...] += (top + jnp.log(total)) - target + jnp.zeros_like(loss_acc)
                dz[at, :] = (expo / total - jnp.where(onehot, 1.0, 0.0)).astype(dz.dtype)
                dz_copy(way, c).start()

        c2 = s - LAG * last - LAG * (last - pos)

        @pl.when((c2 >= 0) & (c2 < chunks) & (pos < last))
        def _():
            dz_copy(way, c2).wait_recv()

            @pl.when(pos > 0)
            def _():
                dz_copy(way, c2).start()

        return carry

    lax.fori_loop(0, 2 * (chunks + 2 * LAG * last), step, 0)

    loss_mine[...] = jnp.broadcast_to(jnp.sum(loss_acc[...], axis=0, keepdims=True), (8, 128))

    def lp_copy(k):
        return pltpu.make_async_remote_copy(
            src_ref=loss_mine,
            dst_ref=loss_plane.at[me],
            send_sem=lp_send.at[k],
            recv_sem=lp_recv.at[k],
            device_id={"proto": lax.rem(me + k, groups)},
            device_id_type=MESH,
        )

    for k in range(1, groups):
        lp_copy(k).start()

    wide = min(256, cols)
    for j in range(cols // wide):
        out = lax.dot_general(
            dz[:, j * wide : (j + 1) * wide],
            emb[...],
            (((0,), (0,)), ((), ())),
            preferred_element_type=jnp.float32,
        ).astype(piece.dtype)
        for t in range(wide // TILE):
            piece[j * (wide // TILE) + t] = out[t * TILE : (t + 1) * TILE, :]

    def ret_copy(k):
        to = lax.rem(me + k, groups)
        return pltpu.make_async_remote_copy(
            src_ref=ret.at[pl.ds(to * CAP, CAP)],
            dst_ref=returned.at[pl.ds(me * CAP, CAP)],
            send_sem=ret_send.at[k],
            recv_sem=ret_recv.at[k],
            device_id={"proto": to},
            device_id_type=MESH,
        )

    for k in range(1, groups):
        to = lax.rem(me + k, groups)
        for t in range(CAP):
            ret[to * CAP + t] = piece[back_ref[to * CAP + t]]
        ret_copy(k).start()
    for t in range(CAP):
        ret[me * CAP + t] = piece[back_ref[me * CAP + t]]
    own_ret = pltpu.make_async_copy(
        ret.at[pl.ds(me * CAP, CAP)], returned.at[pl.ds(me * CAP, CAP)], own_ret_sem
    )
    own_ret.start()

    def grad_block(i, carry):
        at = pl.ds(pl.multiple_of(i * block, block), block)
        grad_emb[at, :] = jnp.dot(
            dz[at, :], tiles[...], preferred_element_type=jnp.float32
        ).astype(grad_emb.dtype)
        return carry

    lax.fori_loop(0, rows // block, grad_block, 0)

    loss_plane[me] = loss_mine[...]
    for k in range(1, groups):
        lp_copy(k).wait()
    plane = loss_plane[0]
    for k in range(1, groups):
        plane = plane + loss_plane[k]
    loss_sum[...] = plane

    def lz_copy(k):
        return pltpu.make_async_remote_copy(
            src_ref=loss_sum,
            dst_ref=loss_z.at[z],
            send_sem=lz_send.at[k],
            recv_sem=lz_recv.at[k],
            device_id={"dp": lax.rem(z + k, dp_count)},
            device_id_type=MESH,
        )

    for k in range(1, dp_count):
        lz_copy(k).start()
    loss_z[z] = plane
    for k in range(1, dp_count):
        lz_copy(k).wait()
    whole = loss_z[0]
    for k in range(1, dp_count):
        whole = whole + loss_z[k]
    loss_out[...] = whole

    def drain(i, carry):
        way = lax.rem(i, 2)
        c = i // 2
        pos = jnp.where(way == 0, z, last - z)

        @pl.when(pos < last)
        def _():
            part_copy(way, c, False).wait_send()

        @pl.when(pos > 0)
        def _():
            dz_copy(way, c).wait_send()

        return carry

    lax.fori_loop(0, 2 * chunks, drain, 0)
    own_ret.wait()
    for k in range(1, groups):
        ret_copy(k).wait()


def fused_body(embeddings, table, tile_lists, labels):
    block_rows, width = embeddings.shape
    list_len = tile_lists.shape[1]
    tiles_here = table.shape[0] // TILE
    groups = lax.axis_size("proto")
    dp_count = lax.axis_size("dp")
    total_rows = block_rows * groups
    cols = list_len * TILE
    slots = groups * CAP
    me = lax.axis_index("proto")
    owners, local, rank = slot_plan(tile_lists, tiles_here)
    match = (owners == me)[:, :, None] & (
        rank[:, :, None] == jnp.arange(CAP, dtype=jnp.int32)[None, None, :]
    )
    select = jnp.sum(match.astype(jnp.int32) * local[:, :, None], axis=1).reshape(-1)
    taken = jnp.any(match, axis=1).reshape(-1)
    my_ids = lax.dynamic_index_in_dim(tile_lists, me, 0, keepdims=False)
    flat = owners * CAP + rank
    my_slot = lax.dynamic_index_in_dim(flat, me, 0, keepdims=False)
    order = jnp.arange(list_len, dtype=jnp.int32)
    back = jnp.sum(
        (my_slot[None, :] == jnp.arange(slots, dtype=jnp.int32)[:, None]).astype(jnp.int32)
        * order[None, :],
        axis=1,
    )
    hit = (my_ids[None, :] == (labels // TILE)[:, None]).astype(jnp.int32)
    column = (jnp.sum(hit * (order * TILE)[None, :], axis=1) + labels % TILE)[:, None]
    outgoing = pack_tiles(table.reshape(tiles_here, TILE, width), select)
    chunks = block_rows // 2 // CHUNK
    bf16, f32 = jnp.bfloat16, jnp.float32
    dma = pltpu.SemaphoreType.DMA
    vmem = pl.BlockSpec(memory_space=pltpu.VMEM)
    smem = pl.BlockSpec(memory_space=pltpu.SMEM)
    hbm = pl.BlockSpec(memory_space=pl.ANY)
    grad_emb, returned, loss = pl.pallas_call(
        functools.partial(main_kernel, groups, dp_count, 1.0 / math.sqrt(D)),
        out_shape=(
            jax.ShapeDtypeStruct((block_rows, width), bf16),
            jax.ShapeDtypeStruct((slots, TILE, width), bf16),
            jax.ShapeDtypeStruct((8, 128), f32),
        ),
        in_specs=[smem, smem, hbm, vmem, vmem],
        out_specs=(vmem, hbm, vmem),
        scratch_shapes=[
            pltpu.VMEM((slots, TILE, width), bf16),
            pltpu.VMEM((cols, width), bf16),
            pltpu.VMEM((block_rows, cols), f32),
            pltpu.VMEM((2, block_rows // 2, cols), f32),
            pltpu.VMEM((block_rows, cols), bf16),
            pltpu.VMEM((list_len, TILE, width), bf16),
            pltpu.VMEM((slots, TILE, width), bf16),
            pltpu.VMEM((CHUNK, 128), f32),
            pltpu.VMEM((8, 128), f32),
            pltpu.VMEM((groups, 8, 128), f32),
            pltpu.VMEM((8, 128), f32),
            pltpu.VMEM((dp_count, 8, 128), f32),
            dma((groups,)),
            dma((groups,)),
            dma,
            dma((2, chunks)),
            dma((2, chunks)),
            dma((2, chunks)),
            dma((2, chunks)),
            dma((groups,)),
            dma((groups,)),
            dma,
            dma((groups,)),
            dma((groups,)),
            dma((dp_count,)),
            dma((dp_count,)),
        ],
        compiler_params=pltpu.CompilerParams(
            collective_id=0, has_side_effects=True, vmem_limit_bytes=VMEM_LIMIT
        ),
    )(my_slot, back, outgoing, embeddings, column)
    grad_table = place_tiles(returned, jnp.where(taken, select, -1), tiles_here)
    return (loss[0, 0] / total_rows, grad_emb, grad_table.reshape(tiles_here * TILE, width))


def fused_bytes(block_rows, width, list_len, groups):
    cols = list_len * TILE
    slots = groups * CAP
    return (
        block_rows * cols * (4 + 4 + 2)
        + 2 * slots * TILE * width * 2
        + 2 * cols * width * 2
        + 2 * block_rows * width * 2
        + block_rows * 128 * 4
    )


def any_body(embeddings, table, tile_lists, labels):
    need = fused_bytes(*embeddings.shape, tile_lists.shape[1], lax.axis_size("proto"))
    if need + 12 * 2**20 <= VMEM_LIMIT:
        return fused_body(embeddings, table, tile_lists, labels)
    return body(embeddings, table, tile_lists, labels)


def solution(mesh):
    placed = (P("proto", "dp"), P("proto", "dp"), P(), P("proto"))
    return jax.shard_map(
        any_body,
        mesh=mesh,
        in_specs=placed,
        out_specs=(P(), P("proto", "dp"), P("proto", "dp")),
        check_vma=False,
    )
```

```python
import functools
import math

import jax
import jax.numpy as jnp
from jax import lax
from jax.experimental import pallas as pl
from jax.experimental.pallas import tpu as pltpu
from jax.sharding import PartitionSpec as P

D = 2560
TILE = 128
CAP = 2
CHUNK = 32
HALF = TILE // 2
LAG = 2
VMEM_LIMIT = 56 * 2**20
MESH = pl.DeviceIdType.MESH


def slot_plan(ids, tiles_here):
    owners = ids // tiles_here
    local = ids % tiles_here
    count = ids.shape[-1]
    before = jnp.arange(count)[:, None] > jnp.arange(count)[None, :]
    earlier = (owners[..., :, None] == owners[..., None, :]) & before
    rank = jnp.sum(earlier.astype(jnp.int32), axis=-1)
    return (owners, local, rank)


def softmax_terms(scores, ids, lab, list_len):
    hit = (ids[None, :] == (lab // TILE)[:, None]).astype(jnp.int32)
    column = (
        jnp.sum(hit * (jnp.arange(list_len, dtype=jnp.int32) * TILE)[None, :], axis=1) + lab % TILE
    )
    onehot = (jnp.arange(list_len * TILE, dtype=jnp.int32)[None, :] == column[:, None]).astype(
        jnp.float32
    )
    top = jnp.max(scores, axis=1, keepdims=True)
    expo = jnp.exp(scores - top)
    total = jnp.sum(expo, axis=1, keepdims=True)
    lse = top[:, 0] + jnp.log(total[:, 0])
    target = jnp.sum(scores * onehot, axis=1)
    dz_rows = (expo / total - onehot).astype(jnp.bfloat16)
    return (jnp.sum(lse - target), dz_rows)


def body(embeddings, table, tile_lists, labels):
    block_rows, width = embeddings.shape
    list_len = tile_lists.shape[1]
    tiles_here = table.shape[0] // TILE
    groups = lax.axis_size("proto")
    dp_count = lax.axis_size("dp")
    rows_dev = block_rows // dp_count
    total_rows = block_rows * groups
    me = lax.axis_index("proto")
    part = lax.axis_index("dp")
    inv_scale = 1.0 / math.sqrt(D)
    owners, local, rank = slot_plan(tile_lists, tiles_here)
    match = (owners == me)[:, :, None] & (
        rank[:, :, None] == jnp.arange(CAP, dtype=jnp.int32)[None, None, :]
    )
    select = jnp.sum(match.astype(jnp.int32) * local[:, :, None], axis=1)
    shaped_table = table.reshape(tiles_here, TILE, width)
    outgoing = pack_tiles(shaped_table, select.reshape(-1)).reshape(groups, CAP, TILE, width)
    incoming = lax.all_to_all(outgoing, "proto", split_axis=0, concat_axis=0, tiled=True)
    my_ids = lax.dynamic_index_in_dim(tile_lists, me, 0, keepdims=False)
    my_owner = lax.dynamic_index_in_dim(owners, me, 0, keepdims=False)
    my_rank = lax.dynamic_index_in_dim(rank, me, 0, keepdims=False)
    flat_slot = my_owner * CAP + my_rank
    tiles = pack_tiles(incoming.reshape(groups * CAP, TILE, width), flat_slot).reshape(
        list_len * TILE, width
    )
    scores = (
        lax.psum_scatter(
            lax.dot_general(
                embeddings, tiles, (((1,), (1,)), ((), ())), preferred_element_type=jnp.float32
            ),
            "dp",
            scatter_dimension=0,
            tiled=True,
        )
        * inv_scale
    )
    my_labels = lax.dynamic_slice_in_dim(labels, part * rows_dev, rows_dev, 0)
    loss_part, dz_rows = softmax_terms(scores, my_ids, my_labels, list_len)
    dz_block = lax.all_gather(dz_rows, "dp", axis=0, tiled=True)
    loss = lax.psum(loss_part, ("dp", "proto")) / total_rows
    grad_emb = jnp.dot(dz_block, tiles, preferred_element_type=jnp.float32).astype(jnp.bfloat16)
    piece = lax.dot_general(
        dz_block, embeddings, (((0,), (0,)), ((), ())), preferred_element_type=jnp.float32
    ).astype(jnp.bfloat16)
    returning = (
        jnp.zeros((groups * CAP, TILE, width), jnp.bfloat16)
        .at[flat_slot]
        .set(piece.reshape(list_len, TILE, width))
    )
    returned = lax.all_to_all(
        returning.reshape(groups, CAP, TILE, width),
        "proto",
        split_axis=0,
        concat_axis=0,
        tiled=True,
    )
    accum = (
        jnp.zeros((tiles_here, TILE, width), jnp.float32)
        .at[select.reshape(-1)]
        .add(returned.reshape(groups * CAP, TILE, width))
    )
    grad_table = accum.reshape(tiles_here * TILE, width).astype(jnp.bfloat16)
    return (loss, grad_emb, grad_table)


def pack_kernel(pick_ref, table_ref, out_ref, sems):
    count = out_ref.shape[0]

    def copy(slot):
        return pltpu.make_async_copy(
            table_ref.at[pick_ref[slot]], out_ref.at[slot], sems.at[slot]
        )

    for slot in range(count):
        copy(slot).start()
    for slot in range(count):
        copy(slot).wait()


def pack_tiles(shaped_table, pick):
    count = pick.shape[0]
    _, tile, width = shaped_table.shape
    return pl.pallas_call(
        pack_kernel,
        out_shape=jax.ShapeDtypeStruct((count, tile, width), shaped_table.dtype),
        grid_spec=pltpu.PrefetchScalarGridSpec(
            num_scalar_prefetch=1,
            grid=(1,),
            in_specs=[pl.BlockSpec(memory_space=pl.ANY)],
            out_specs=pl.BlockSpec(memory_space=pltpu.VMEM),
            scratch_shapes=[pltpu.SemaphoreType.DMA((count,))],
        ),
        compiler_params=pltpu.CompilerParams(vmem_limit_bytes=32 * 2**20),
    )(pick, shaped_table)


def place_kernel(per_step, count, pick_ref, uses_ref, first_ref, got_ref, emb_in, out_ref, emb_out, acc_ref):
    step = pl.program_id(0)
    emb_out[...] = emb_in[...]
    for inner in range(per_step):
        tile_id = step * per_step + inner
        uses = uses_ref[tile_id]

        @pl.when(uses == 0)
        def _():
            out_ref[inner] = jnp.zeros(out_ref.shape[1:], out_ref.dtype)

        @pl.when(uses == 1)
        def _():
            out_ref[inner] = got_ref[first_ref[tile_id]]

        @pl.when(uses > 1)
        def _():
            acc_ref[...] = jnp.zeros_like(acc_ref)

            def add(slot, carry):
                @pl.when(pick_ref[slot] == tile_id)
                def _():
                    acc_ref[...] += got_ref[slot].astype(jnp.float32)

                return carry

            lax.fori_loop(0, count, add, 0)
            out_ref[inner] = acc_ref[...].astype(out_ref.dtype)


def place_tiles(returned, pick, grad_emb, tiles_here):
    count, tile, width = returned.shape
    per_step = 4
    steps = tiles_here // per_step
    emb_spec = pl.BlockSpec((grad_emb.shape[0] // steps, width), lambda i, *refs: (i, 0))
    named = pick[None, :] == jnp.arange(tiles_here, dtype=jnp.int32)[:, None]
    uses = jnp.sum(named.astype(jnp.int32), axis=1)
    first = jnp.max(named * jnp.arange(count, dtype=jnp.int32)[None, :], axis=1)
    return pl.pallas_call(
        functools.partial(place_kernel, per_step, count),
        out_shape=(
            jax.ShapeDtypeStruct((tiles_here, tile, width), returned.dtype),
            jax.ShapeDtypeStruct(grad_emb.shape, grad_emb.dtype),
        ),
        grid_spec=pltpu.PrefetchScalarGridSpec(
            num_scalar_prefetch=3,
            grid=(steps,),
            in_specs=[pl.BlockSpec(memory_space=pltpu.VMEM), emb_spec],
            out_specs=(
                pl.BlockSpec((per_step, tile, width), lambda i, *refs: (i, 0, 0)),
                emb_spec,
            ),
            scratch_shapes=[pltpu.VMEM((tile, width), jnp.float32)],
        ),
        compiler_params=pltpu.CompilerParams(vmem_limit_bytes=24 * 2**20),
    )(pick, uses, first, returned, grad_emb)


def main_kernel(
    groups,
    dp_count,
    inv_scale,
    slot_ref,
    back_ref,
    out_tiles,
    emb,
    column,
    grad_emb,
    returned,
    loss_out,
    incoming_a,
    incoming_b,
    tiles,
    scores,
    partial,
    dz,
    piece,
    ret,
    loss_acc,
    loss_mine,
    loss_plane,
    loss_sum,
    loss_z,
    tile_send,
    tile_recv,
    own_sem,
    part_send,
    part_recv,
    dz_send,
    dz_recv,
    ret_send,
    ret_recv,
    own_ret_sem,
    lp_send,
    lp_recv,
    lz_send,
    lz_recv,
):
    me = lax.axis_index("proto")
    z = lax.axis_index("dp")
    rows, width = emb.shape
    list_len = slot_ref.shape[0]
    cols = list_len * TILE
    half = rows // 2
    chunks = half // CHUNK
    part_cols = cols // 2
    incoming = (incoming_a, incoming_b)
    last = dp_count - 1

    barrier = pltpu.get_barrier_semaphore()
    for k in range(1, groups):
        pl.semaphore_signal(
            barrier, inc=1, device_id={"proto": lax.rem(me + k, groups)}, device_id_type=MESH
        )
    for k in range(1, dp_count):
        pl.semaphore_signal(
            barrier, inc=1, device_id={"dp": lax.rem(z + k, dp_count)}, device_id_type=MESH
        )
    pl.semaphore_wait(barrier, groups + dp_count - 2)

    def tile_copy(h, k):
        to = lax.rem(me + k, groups)
        return pltpu.make_async_remote_copy(
            src_ref=out_tiles.at[pl.ds(to * CAP, CAP), pl.ds(h * HALF, HALF)],
            dst_ref=incoming[h].at[pl.ds(me * CAP, CAP)],
            send_sem=tile_send.at[h, k],
            recv_sem=tile_recv.at[h, k],
            device_id={"proto": to},
            device_id_type=MESH,
        )

    def own_copy(h):
        return pltpu.make_async_copy(
            out_tiles.at[pl.ds(me * CAP, CAP), pl.ds(h * HALF, HALF)],
            incoming[h].at[pl.ds(me * CAP, CAP)],
            own_sem.at[h],
        )

    def tiles_in(h):
        own_copy(h).wait()
        for k in range(1, groups):
            tile_copy(h, k).wait()
        for j in range(list_len):
            at = h * part_cols + j * HALF
            tiles[at : at + HALF, :] = incoming[h][slot_ref[j]]

    for h in range(2):
        for k in range(1, groups):
            tile_copy(h, k).start()
        own_copy(h).start()
    loss_acc[...] = jnp.zeros_like(loss_acc)
    tiles_in(0)

    block = min(256, half)
    group = 128 // CHUNK

    def rows_of(way, c):
        return pl.multiple_of((1 - way) * half + c * CHUNK, CHUNK)

    def part_copy(way, h, c, first):
        lanes = pl.ds(pl.multiple_of(h * part_cols, part_cols), part_cols)
        dst = partial.at[way, pl.ds(pl.multiple_of(c * CHUNK, CHUNK), CHUNK), lanes]
        src = scores.at[pl.ds(rows_of(way, c), CHUNK), lanes] if first else dst
        return pltpu.make_async_remote_copy(
            src_ref=src,
            dst_ref=dst,
            send_sem=part_send.at[way, h, c],
            recv_sem=part_recv.at[way, h, c],
            device_id={"dp": jnp.clip(z + 1 - 2 * way, 0, last)},
            device_id_type=MESH,
        )

    def dz_copy(way, c):
        at = dz.at[pl.ds(rows_of(way, c), CHUNK)]
        return pltpu.make_async_remote_copy(
            src_ref=at,
            dst_ref=at,
            send_sem=dz_send.at[way, c],
            recv_sem=dz_recv.at[way, c],
            device_id={"dp": jnp.clip(z - 1 + 2 * way, 0, last)},
            device_id_type=MESH,
        )

    lane = lax.broadcasted_iota(jnp.int32, (CHUNK, cols), 1)

    def step(i, carry):
        way = lax.rem(i, 2)
        s = i // 2
        pos = jnp.where(way == 0, z, last - z)
        turn = s - LAG * pos

        @pl.when((turn >= 0) & (turn < 2 * chunks))
        def _():
            h = turn // chunks
            c = lax.rem(turn, chunks)
            lanes = pl.ds(pl.multiple_of(h * part_cols, part_cols), part_cols)

            @pl.when(lax.rem(c, group) == 0)
            def _():
                these = pl.ds(rows_of(way, c), group * CHUNK)
                scores[these, lanes] = lax.dot_general(
                    emb[these, :],
                    tiles[lanes, :],
                    (((1,), (1,)), ((), ())),
                    preferred_element_type=jnp.float32,
                )

            at = pl.ds(rows_of(way, c), CHUNK)
            here = pl.ds(pl.multiple_of(c * CHUNK, CHUNK), CHUNK)

            @pl.when(pos == 0)
            def _():
                part_copy(way, h, c, True).start()

            @pl.when((pos > 0) & (pos < last))
            def _():
                part_copy(way, h, c, False).wait_recv()
                partial[way, here, lanes] += scores[at, lanes]
                part_copy(way, h, c, False).start()

            @pl.when((pos == last) & (h == 1))
            def _():
                part_copy(way, 0, c, False).wait_recv()
                part_copy(way, 1, c, False).wait_recv()
                score = (partial[way, here, :] + scores[at, :]) * inv_scale
                onehot = lane == column[at, :]
                top = jnp.max(score, axis=1, keepdims=True)
                expo = jnp.exp(score - top)
                total = jnp.sum(expo, axis=1, keepdims=True)
                target = jnp.sum(jnp.where(onehot, score, 0.0), axis=1, keepdims=True)
                loss_acc[...] += (top + jnp.log(total)) - target + jnp.zeros_like(loss_acc)
                dz[at, :] = (expo / total - jnp.where(onehot, 1.0, 0.0)).astype(dz.dtype)
                dz_copy(way, c).start()

        c2 = s - chunks - LAG * last - LAG * (last - pos)

        @pl.when((c2 >= 0) & (c2 < chunks) & (pos < last))
        def _():
            dz_copy(way, c2).wait_recv()

            @pl.when(pos > 0)
            def _():
                dz_copy(way, c2).start()

        return carry

    lax.fori_loop(0, 2 * chunks, step, 0)
    tiles_in(1)
    lax.fori_loop(2 * chunks, 2 * (2 * chunks + 2 * LAG * last), step, 0)

    loss_mine[...] = jnp.broadcast_to(jnp.sum(loss_acc[...], axis=0, keepdims=True), (8, 128))

    def lp_copy(k):
        return pltpu.make_async_remote_copy(
            src_ref=loss_mine,
            dst_ref=loss_plane.at[me],
            send_sem=lp_send.at[k],
            recv_sem=lp_recv.at[k],
            device_id={"proto": lax.rem(me + k, groups)},
            device_id_type=MESH,
        )

    for k in range(1, groups):
        lp_copy(k).start()

    wide = min(256, cols)
    for j in range(cols // wide):
        out = lax.dot_general(
            dz[:, j * wide : (j + 1) * wide],
            emb[...],
            (((0,), (0,)), ((), ())),
            preferred_element_type=jnp.float32,
        ).astype(piece.dtype)
        for t in range(wide // HALF):
            h, tile = divmod(j * (wide // HALF) + t, list_len)
            piece[tile, h * HALF : (h + 1) * HALF, :] = out[t * HALF : (t + 1) * HALF, :]

    def ret_copy(k):
        to = lax.rem(me + k, groups)
        return pltpu.make_async_remote_copy(
            src_ref=ret.at[pl.ds(to * CAP, CAP)],
            dst_ref=returned.at[pl.ds(me * CAP, CAP)],
            send_sem=ret_send.at[k],
            recv_sem=ret_recv.at[k],
            device_id={"proto": to},
            device_id_type=MESH,
        )

    for k in range(1, groups):
        to = lax.rem(me + k, groups)
        for t in range(CAP):
            ret[to * CAP + t] = piece[back_ref[to * CAP + t]]
        ret_copy(k).start()
    for t in range(CAP):
        ret[me * CAP + t] = piece[back_ref[me * CAP + t]]
    own_ret = pltpu.make_async_copy(
        ret.at[pl.ds(me * CAP, CAP)], returned.at[pl.ds(me * CAP, CAP)], own_ret_sem
    )
    own_ret.start()

    def grad_block(i, carry):
        at = pl.ds(pl.multiple_of(i * block, block), block)
        grad_emb[at, :] = jnp.dot(
            dz[at, :], tiles[...], preferred_element_type=jnp.float32
        ).astype(grad_emb.dtype)
        return carry

    lax.fori_loop(0, rows // block, grad_block, 0)

    loss_plane[me] = loss_mine[...]
    for k in range(1, groups):
        lp_copy(k).wait()
    plane = loss_plane[0]
    for k in range(1, groups):
        plane = plane + loss_plane[k]
    loss_sum[...] = plane

    def lz_copy(k):
        return pltpu.make_async_remote_copy(
            src_ref=loss_sum,
            dst_ref=loss_z.at[z],
            send_sem=lz_send.at[k],
            recv_sem=lz_recv.at[k],
            device_id={"dp": lax.rem(z + k, dp_count)},
            device_id_type=MESH,
        )

    for k in range(1, dp_count):
        lz_copy(k).start()
    loss_z[z] = plane
    for k in range(1, dp_count):
        lz_copy(k).wait()
    whole = loss_z[0]
    for k in range(1, dp_count):
        whole = whole + loss_z[k]
    loss_out[...] = whole

    def drain(i, carry):
        way = lax.rem(i, 2)
        c = i // 2
        pos = jnp.where(way == 0, z, last - z)

        @pl.when(pos < last)
        def _():
            part_copy(way, 0, c, False).wait_send()
            part_copy(way, 1, c, False).wait_send()

        @pl.when(pos > 0)
        def _():
            dz_copy(way, c).wait_send()

        return carry

    lax.fori_loop(0, 2 * chunks, drain, 0)
    own_ret.wait()
    for k in range(1, groups):
        ret_copy(k).wait()


def fused_body(embeddings, table, tile_lists, labels):
    block_rows, width = embeddings.shape
    list_len = tile_lists.shape[1]
    tiles_here = table.shape[0] // TILE
    groups = lax.axis_size("proto")
    dp_count = lax.axis_size("dp")
    total_rows = block_rows * groups
    cols = list_len * TILE
    slots = groups * CAP
    me = lax.axis_index("proto")
    owners, local, rank = slot_plan(tile_lists, tiles_here)
    match = (owners == me)[:, :, None] & (
        rank[:, :, None] == jnp.arange(CAP, dtype=jnp.int32)[None, None, :]
    )
    select = jnp.sum(match.astype(jnp.int32) * local[:, :, None], axis=1).reshape(-1)
    taken = jnp.any(match, axis=1).reshape(-1)
    my_ids = lax.dynamic_index_in_dim(tile_lists, me, 0, keepdims=False)
    flat = owners * CAP + rank
    my_slot = lax.dynamic_index_in_dim(flat, me, 0, keepdims=False)
    order = jnp.arange(list_len, dtype=jnp.int32)
    back = jnp.sum(
        (my_slot[None, :] == jnp.arange(slots, dtype=jnp.int32)[:, None]).astype(jnp.int32)
        * order[None, :],
        axis=1,
    )
    hit = (my_ids[None, :] == (labels // TILE)[:, None]).astype(jnp.int32)
    within = labels % TILE
    column = (
        jnp.sum(hit * (order * HALF)[None, :], axis=1)
        + within // HALF * (cols // 2)
        + within % HALF
    )[:, None]
    outgoing = pack_tiles(table.reshape(tiles_here, TILE, width), select)
    chunks = block_rows // 2 // CHUNK
    bf16, f32 = jnp.bfloat16, jnp.float32
    dma = pltpu.SemaphoreType.DMA
    vmem = pl.BlockSpec(memory_space=pltpu.VMEM)
    smem = pl.BlockSpec(memory_space=pltpu.SMEM)
    hbm = pl.BlockSpec(memory_space=pl.ANY)
    grad_emb, returned, loss = pl.pallas_call(
        functools.partial(main_kernel, groups, dp_count, 1.0 / math.sqrt(D)),
        out_shape=(
            jax.ShapeDtypeStruct((block_rows, width), bf16),
            jax.ShapeDtypeStruct((slots, TILE, width), bf16),
            jax.ShapeDtypeStruct((8, 128), f32),
        ),
        in_specs=[smem, smem, hbm, vmem, vmem],
        out_specs=(vmem, hbm, vmem),
        scratch_shapes=[
            pltpu.VMEM((slots, HALF, width), bf16),
            pltpu.VMEM((slots, HALF, width), bf16),
            pltpu.VMEM((cols, width), bf16),
            pltpu.VMEM((block_rows, cols), f32),
            pltpu.VMEM((2, block_rows // 2, cols), f32),
            pltpu.VMEM((block_rows, cols), bf16),
            pltpu.VMEM((list_len, TILE, width), bf16),
            pltpu.VMEM((slots, TILE, width), bf16),
            pltpu.VMEM((CHUNK, 128), f32),
            pltpu.VMEM((8, 128), f32),
            pltpu.VMEM((groups, 8, 128), f32),
            pltpu.VMEM((8, 128), f32),
            pltpu.VMEM((dp_count, 8, 128), f32),
            dma((2, groups)),
            dma((2, groups)),
            dma((2,)),
            dma((2, 2, chunks)),
            dma((2, 2, chunks)),
            dma((2, chunks)),
            dma((2, chunks)),
            dma((groups,)),
            dma((groups,)),
            dma,
            dma((groups,)),
            dma((groups,)),
            dma((dp_count,)),
            dma((dp_count,)),
        ],
        compiler_params=pltpu.CompilerParams(
            collective_id=0, has_side_effects=True, vmem_limit_bytes=VMEM_LIMIT
        ),
    )(my_slot, back, outgoing, embeddings, column)
    grad_table, grad_emb = place_tiles(
        returned, jnp.where(taken, select, -1), grad_emb, tiles_here
    )
    return (loss[0, 0] / total_rows, grad_emb, grad_table.reshape(tiles_here * TILE, width))


def fused_bytes(block_rows, width, list_len, groups):
    cols = list_len * TILE
    slots = groups * CAP
    return (
        block_rows * cols * (4 + 4 + 2)
        + 2 * slots * TILE * width * 2
        + 2 * cols * width * 2
        + 2 * block_rows * width * 2
        + block_rows * 128 * 4
    )


def any_body(embeddings, table, tile_lists, labels):
    need = fused_bytes(*embeddings.shape, tile_lists.shape[1], lax.axis_size("proto"))
    if need + 12 * 2**20 <= VMEM_LIMIT:
        return fused_body(embeddings, table, tile_lists, labels)
    return body(embeddings, table, tile_lists, labels)


def solution(mesh):
    placed = (P("proto", "dp"), P("proto", "dp"), P(), P("proto"))
    return jax.shard_map(
        any_body,
        mesh=mesh,
        in_specs=placed,
        out_specs=(P(), P("proto", "dp"), P("proto", "dp")),
        check_vma=False,
    )
```

```python
import functools
import math

import jax
import jax.numpy as jnp
from jax import lax
from jax.experimental import pallas as pl
from jax.experimental.pallas import tpu as pltpu
from jax.sharding import PartitionSpec as P

D = 2560
TILE = 128
CAP = 2
CHUNK = 32
HALF = TILE // 2
LAG = 2
VMEM_LIMIT = 56 * 2**20
MESH = pl.DeviceIdType.MESH


def slot_plan(ids, tiles_here):
    owners = ids // tiles_here
    local = ids % tiles_here
    count = ids.shape[-1]
    before = jnp.arange(count)[:, None] > jnp.arange(count)[None, :]
    earlier = (owners[..., :, None] == owners[..., None, :]) & before
    rank = jnp.sum(earlier.astype(jnp.int32), axis=-1)
    return (owners, local, rank)


def softmax_terms(scores, ids, lab, list_len):
    hit = (ids[None, :] == (lab // TILE)[:, None]).astype(jnp.int32)
    column = (
        jnp.sum(hit * (jnp.arange(list_len, dtype=jnp.int32) * TILE)[None, :], axis=1) + lab % TILE
    )
    onehot = (jnp.arange(list_len * TILE, dtype=jnp.int32)[None, :] == column[:, None]).astype(
        jnp.float32
    )
    top = jnp.max(scores, axis=1, keepdims=True)
    expo = jnp.exp(scores - top)
    total = jnp.sum(expo, axis=1, keepdims=True)
    lse = top[:, 0] + jnp.log(total[:, 0])
    target = jnp.sum(scores * onehot, axis=1)
    dz_rows = (expo / total - onehot).astype(jnp.bfloat16)
    return (jnp.sum(lse - target), dz_rows)


def body(embeddings, table, tile_lists, labels):
    block_rows, width = embeddings.shape
    list_len = tile_lists.shape[1]
    tiles_here = table.shape[0] // TILE
    groups = lax.axis_size("proto")
    dp_count = lax.axis_size("dp")
    rows_dev = block_rows // dp_count
    total_rows = block_rows * groups
    me = lax.axis_index("proto")
    part = lax.axis_index("dp")
    inv_scale = 1.0 / math.sqrt(D)
    owners, local, rank = slot_plan(tile_lists, tiles_here)
    match = (owners == me)[:, :, None] & (
        rank[:, :, None] == jnp.arange(CAP, dtype=jnp.int32)[None, None, :]
    )
    select = jnp.sum(match.astype(jnp.int32) * local[:, :, None], axis=1)
    shaped_table = table.reshape(tiles_here, TILE, width)
    outgoing = pack_tiles(shaped_table, select.reshape(-1)).reshape(groups, CAP, TILE, width)
    incoming = lax.all_to_all(outgoing, "proto", split_axis=0, concat_axis=0, tiled=True)
    my_ids = lax.dynamic_index_in_dim(tile_lists, me, 0, keepdims=False)
    my_owner = lax.dynamic_index_in_dim(owners, me, 0, keepdims=False)
    my_rank = lax.dynamic_index_in_dim(rank, me, 0, keepdims=False)
    flat_slot = my_owner * CAP + my_rank
    tiles = pack_tiles(incoming.reshape(groups * CAP, TILE, width), flat_slot).reshape(
        list_len * TILE, width
    )
    scores = (
        lax.psum_scatter(
            lax.dot_general(
                embeddings, tiles, (((1,), (1,)), ((), ())), preferred_element_type=jnp.float32
            ),
            "dp",
            scatter_dimension=0,
            tiled=True,
        )
        * inv_scale
    )
    my_labels = lax.dynamic_slice_in_dim(labels, part * rows_dev, rows_dev, 0)
    loss_part, dz_rows = softmax_terms(scores, my_ids, my_labels, list_len)
    dz_block = lax.all_gather(dz_rows, "dp", axis=0, tiled=True)
    loss = lax.psum(loss_part, ("dp", "proto")) / total_rows
    grad_emb = jnp.dot(dz_block, tiles, preferred_element_type=jnp.float32).astype(jnp.bfloat16)
    piece = lax.dot_general(
        dz_block, embeddings, (((0,), (0,)), ((), ())), preferred_element_type=jnp.float32
    ).astype(jnp.bfloat16)
    returning = (
        jnp.zeros((groups * CAP, TILE, width), jnp.bfloat16)
        .at[flat_slot]
        .set(piece.reshape(list_len, TILE, width))
    )
    returned = lax.all_to_all(
        returning.reshape(groups, CAP, TILE, width),
        "proto",
        split_axis=0,
        concat_axis=0,
        tiled=True,
    )
    accum = (
        jnp.zeros((tiles_here, TILE, width), jnp.float32)
        .at[select.reshape(-1)]
        .add(returned.reshape(groups * CAP, TILE, width))
    )
    grad_table = accum.reshape(tiles_here * TILE, width).astype(jnp.bfloat16)
    return (loss, grad_emb, grad_table)


def pack_kernel(pick_ref, table_ref, out_ref, sems):
    count = out_ref.shape[0]

    def copy(slot):
        return pltpu.make_async_copy(
            table_ref.at[pick_ref[slot]], out_ref.at[slot], sems.at[slot]
        )

    for slot in range(count):
        copy(slot).start()
    for slot in range(count):
        copy(slot).wait()


def pack_tiles(shaped_table, pick):
    count = pick.shape[0]
    _, tile, width = shaped_table.shape
    return pl.pallas_call(
        pack_kernel,
        out_shape=jax.ShapeDtypeStruct((count, tile, width), shaped_table.dtype),
        grid_spec=pltpu.PrefetchScalarGridSpec(
            num_scalar_prefetch=1,
            grid=(1,),
            in_specs=[pl.BlockSpec(memory_space=pl.ANY)],
            out_specs=pl.BlockSpec(memory_space=pltpu.VMEM),
            scratch_shapes=[pltpu.SemaphoreType.DMA((count,))],
        ),
        compiler_params=pltpu.CompilerParams(vmem_limit_bytes=32 * 2**20),
    )(pick, shaped_table)


def place_kernel(per_step, count, pick_ref, uses_ref, first_ref, got_ref, emb_in, out_ref, emb_out, acc_ref):
    step = pl.program_id(0)
    emb_out[...] = emb_in[...]
    for inner in range(per_step):
        tile_id = step * per_step + inner
        uses = uses_ref[tile_id]

        @pl.when(uses == 0)
        def _():
            out_ref[inner] = jnp.zeros(out_ref.shape[1:], out_ref.dtype)

        @pl.when(uses == 1)
        def _():
            out_ref[inner] = got_ref[first_ref[tile_id]]

        @pl.when(uses > 1)
        def _():
            acc_ref[...] = jnp.zeros_like(acc_ref)

            def add(slot, carry):
                @pl.when(pick_ref[slot] == tile_id)
                def _():
                    acc_ref[...] += got_ref[slot].astype(jnp.float32)

                return carry

            lax.fori_loop(0, count, add, 0)
            out_ref[inner] = acc_ref[...].astype(out_ref.dtype)


def place_tiles(returned, pick, grad_emb, tiles_here):
    count, tile, width = returned.shape
    per_step = 4
    steps = tiles_here // per_step
    emb_spec = pl.BlockSpec((grad_emb.shape[0] // steps, width), lambda i, *refs: (i, 0))
    named = pick[None, :] == jnp.arange(tiles_here, dtype=jnp.int32)[:, None]
    uses = jnp.sum(named.astype(jnp.int32), axis=1)
    first = jnp.max(named * jnp.arange(count, dtype=jnp.int32)[None, :], axis=1)
    return pl.pallas_call(
        functools.partial(place_kernel, per_step, count),
        out_shape=(
            jax.ShapeDtypeStruct((tiles_here, tile, width), returned.dtype),
            jax.ShapeDtypeStruct(grad_emb.shape, grad_emb.dtype),
        ),
        grid_spec=pltpu.PrefetchScalarGridSpec(
            num_scalar_prefetch=3,
            grid=(steps,),
            in_specs=[pl.BlockSpec(memory_space=pltpu.VMEM), emb_spec],
            out_specs=(
                pl.BlockSpec((per_step, tile, width), lambda i, *refs: (i, 0, 0)),
                emb_spec,
            ),
            scratch_shapes=[pltpu.VMEM((tile, width), jnp.float32)],
        ),
        compiler_params=pltpu.CompilerParams(vmem_limit_bytes=VMEM_LIMIT),
    )(pick, uses, first, returned, grad_emb)


def main_kernel(
    groups,
    dp_count,
    inv_scale,
    slot_ref,
    back_ref,
    out_tiles,
    emb,
    column,
    grad_emb,
    returned,
    loss_out,
    incoming_a,
    incoming_b,
    tiles,
    scores,
    partial,
    dz,
    piece,
    ret,
    loss_acc,
    loss_mine,
    loss_plane,
    loss_sum,
    loss_z,
    tile_send,
    tile_recv,
    own_sem,
    part_send,
    part_recv,
    dz_send,
    dz_recv,
    ret_send,
    ret_recv,
    own_ret_sem,
    lp_send,
    lp_recv,
    lz_send,
    lz_recv,
):
    me = lax.axis_index("proto")
    z = lax.axis_index("dp")
    rows, width = emb.shape
    list_len = slot_ref.shape[0]
    cols = list_len * TILE
    half = rows // 2
    chunks = half // CHUNK
    part_cols = cols // 2
    incoming = (incoming_a, incoming_b)
    last = dp_count - 1

    barrier = pltpu.get_barrier_semaphore()
    for k in range(1, groups):
        pl.semaphore_signal(
            barrier, inc=1, device_id={"proto": lax.rem(me + k, groups)}, device_id_type=MESH
        )
    for k in range(1, dp_count):
        pl.semaphore_signal(
            barrier, inc=1, device_id={"dp": lax.rem(z + k, dp_count)}, device_id_type=MESH
        )
    pl.semaphore_wait(barrier, groups + dp_count - 2)

    def tile_copy(h, k):
        to = lax.rem(me + k, groups)
        return pltpu.make_async_remote_copy(
            src_ref=out_tiles.at[pl.ds(to * CAP, CAP), pl.ds(h * HALF, HALF)],
            dst_ref=incoming[h].at[pl.ds(me * CAP, CAP)],
            send_sem=tile_send.at[h, k],
            recv_sem=tile_recv.at[h, k],
            device_id={"proto": to},
            device_id_type=MESH,
        )

    def own_copy(h):
        return pltpu.make_async_copy(
            out_tiles.at[pl.ds(me * CAP, CAP), pl.ds(h * HALF, HALF)],
            incoming[h].at[pl.ds(me * CAP, CAP)],
            own_sem.at[h],
        )

    def tiles_in(h):
        own_copy(h).wait()
        for k in range(1, groups):
            tile_copy(h, k).wait()
        for j in range(list_len):
            at = h * part_cols + j * HALF
            tiles[at : at + HALF, :] = incoming[h][slot_ref[j]]

    for h in range(2):
        for k in range(1, groups):
            tile_copy(h, k).start()
        own_copy(h).start()
    loss_acc[...] = jnp.zeros_like(loss_acc)
    tiles_in(0)

    block = min(256, half)
    group = 128 // CHUNK

    def rows_of(way, c):
        return pl.multiple_of((1 - way) * half + c * CHUNK, CHUNK)

    def part_copy(way, h, c, first):
        lanes = pl.ds(pl.multiple_of(h * part_cols, part_cols), part_cols)
        dst = partial.at[way, pl.ds(pl.multiple_of(c * CHUNK, CHUNK), CHUNK), lanes]
        src = scores.at[pl.ds(rows_of(way, c), CHUNK), lanes] if first else dst
        return pltpu.make_async_remote_copy(
            src_ref=src,
            dst_ref=dst,
            send_sem=part_send.at[way, h, c],
            recv_sem=part_recv.at[way, h, c],
            device_id={"dp": jnp.clip(z + 1 - 2 * way, 0, last)},
            device_id_type=MESH,
        )

    def dz_copy(way, c):
        at = dz.at[pl.ds(rows_of(way, c), CHUNK)]
        return pltpu.make_async_remote_copy(
            src_ref=at,
            dst_ref=at,
            send_sem=dz_send.at[way, c],
            recv_sem=dz_recv.at[way, c],
            device_id={"dp": jnp.clip(z - 1 + 2 * way, 0, last)},
            device_id_type=MESH,
        )

    lane = lax.broadcasted_iota(jnp.int32, (CHUNK, cols), 1)

    def step(i, carry):
        way = lax.rem(i, 2)
        s = i // 2
        pos = jnp.where(way == 0, z, last - z)
        turn = s - LAG * pos

        @pl.when((turn >= 0) & (turn < 2 * chunks))
        def _():
            h = turn // chunks
            c = lax.rem(turn, chunks)
            lanes = pl.ds(pl.multiple_of(h * part_cols, part_cols), part_cols)

            @pl.when(lax.rem(c, group) == 0)
            def _():
                these = pl.ds(rows_of(way, c), group * CHUNK)
                scores[these, lanes] = lax.dot_general(
                    emb[these, :],
                    tiles[lanes, :],
                    (((1,), (1,)), ((), ())),
                    preferred_element_type=jnp.float32,
                )

            at = pl.ds(rows_of(way, c), CHUNK)
            here = pl.ds(pl.multiple_of(c * CHUNK, CHUNK), CHUNK)

            @pl.when(pos == 0)
            def _():
                part_copy(way, h, c, True).start()

            @pl.when((pos > 0) & (pos < last))
            def _():
                part_copy(way, h, c, False).wait_recv()
                partial[way, here, lanes] += scores[at, lanes]
                part_copy(way, h, c, False).start()

            @pl.when((pos == last) & (h == 1))
            def _():
                part_copy(way, 0, c, False).wait_recv()
                part_copy(way, 1, c, False).wait_recv()
                score = (partial[way, here, :] + scores[at, :]) * inv_scale
                onehot = lane == column[at, :]
                top = jnp.max(score, axis=1, keepdims=True)
                expo = jnp.exp(score - top)
                total = jnp.sum(expo, axis=1, keepdims=True)
                target = jnp.sum(jnp.where(onehot, score, 0.0), axis=1, keepdims=True)
                loss_acc[...] += (top + jnp.log(total)) - target + jnp.zeros_like(loss_acc)
                dz[at, :] = (expo / total - jnp.where(onehot, 1.0, 0.0)).astype(dz.dtype)
                dz_copy(way, c).start()

        c2 = s - chunks - LAG * last - LAG * (last - pos)

        @pl.when((c2 >= 0) & (c2 < chunks) & (pos < last))
        def _():
            dz_copy(way, c2).wait_recv()

            @pl.when(pos > 0)
            def _():
                dz_copy(way, c2).start()

        return carry

    lax.fori_loop(0, 2 * chunks, step, 0)
    tiles_in(1)
    lax.fori_loop(2 * chunks, 2 * (2 * chunks + 2 * LAG * last), step, 0)

    loss_mine[...] = jnp.broadcast_to(jnp.sum(loss_acc[...], axis=0, keepdims=True), (8, 128))

    def lp_copy(k):
        return pltpu.make_async_remote_copy(
            src_ref=loss_mine,
            dst_ref=loss_plane.at[me],
            send_sem=lp_send.at[k],
            recv_sem=lp_recv.at[k],
            device_id={"proto": lax.rem(me + k, groups)},
            device_id_type=MESH,
        )

    for k in range(1, groups):
        lp_copy(k).start()

    wide = min(256, part_cols)

    def ret_copy(h, k):
        to = lax.rem(me + k, groups)
        these = pl.ds(h * HALF, HALF)
        return pltpu.make_async_remote_copy(
            src_ref=ret.at[pl.ds(to * CAP, CAP), these],
            dst_ref=returned.at[pl.ds(me * CAP, CAP), these],
            send_sem=ret_send.at[h, k],
            recv_sem=ret_recv.at[h, k],
            device_id={"proto": to},
            device_id_type=MESH,
        )

    for h in range(2):
        these = slice(h * HALF, (h + 1) * HALF)
        for j in range(part_cols // wide):
            at = h * part_cols + j * wide
            out = lax.dot_general(
                dz[:, at : at + wide],
                emb[...],
                (((0,), (0,)), ((), ())),
                preferred_element_type=jnp.float32,
            ).astype(piece.dtype)
            for t in range(wide // HALF):
                piece[j * (wide // HALF) + t, these, :] = out[t * HALF : (t + 1) * HALF, :]
        for k in range(1, groups):
            to = lax.rem(me + k, groups)
            for t in range(CAP):
                ret[to * CAP + t, these, :] = piece[back_ref[to * CAP + t], these, :]
            ret_copy(h, k).start()
    for t in range(CAP):
        ret[me * CAP + t] = piece[back_ref[me * CAP + t]]
    own_ret = pltpu.make_async_copy(
        ret.at[pl.ds(me * CAP, CAP)], returned.at[pl.ds(me * CAP, CAP)], own_ret_sem
    )
    own_ret.start()

    def grad_block(i, carry):
        at = pl.ds(pl.multiple_of(i * block, block), block)
        grad_emb[at, :] = jnp.dot(
            dz[at, :], tiles[...], preferred_element_type=jnp.float32
        ).astype(grad_emb.dtype)
        return carry

    lax.fori_loop(0, rows // block, grad_block, 0)

    loss_plane[me] = loss_mine[...]
    for k in range(1, groups):
        lp_copy(k).wait()
    plane = loss_plane[0]
    for k in range(1, groups):
        plane = plane + loss_plane[k]
    loss_sum[...] = plane

    def lz_copy(k):
        return pltpu.make_async_remote_copy(
            src_ref=loss_sum,
            dst_ref=loss_z.at[z],
            send_sem=lz_send.at[k],
            recv_sem=lz_recv.at[k],
            device_id={"dp": lax.rem(z + k, dp_count)},
            device_id_type=MESH,
        )

    for k in range(1, dp_count):
        lz_copy(k).start()
    loss_z[z] = plane
    for k in range(1, dp_count):
        lz_copy(k).wait()
    whole = loss_z[0]
    for k in range(1, dp_count):
        whole = whole + loss_z[k]
    loss_out[...] = whole

    def drain(i, carry):
        way = lax.rem(i, 2)
        c = i // 2
        pos = jnp.where(way == 0, z, last - z)

        @pl.when(pos < last)
        def _():
            part_copy(way, 0, c, False).wait_send()
            part_copy(way, 1, c, False).wait_send()

        @pl.when(pos > 0)
        def _():
            dz_copy(way, c).wait_send()

        return carry

    lax.fori_loop(0, 2 * chunks, drain, 0)
    own_ret.wait()
    for h in range(2):
        for k in range(1, groups):
            ret_copy(h, k).wait()


def fused_body(embeddings, table, tile_lists, labels):
    block_rows, width = embeddings.shape
    list_len = tile_lists.shape[1]
    tiles_here = table.shape[0] // TILE
    groups = lax.axis_size("proto")
    dp_count = lax.axis_size("dp")
    total_rows = block_rows * groups
    cols = list_len * TILE
    slots = groups * CAP
    me = lax.axis_index("proto")
    owners, local, rank = slot_plan(tile_lists, tiles_here)
    match = (owners == me)[:, :, None] & (
        rank[:, :, None] == jnp.arange(CAP, dtype=jnp.int32)[None, None, :]
    )
    select = jnp.sum(match.astype(jnp.int32) * local[:, :, None], axis=1).reshape(-1)
    taken = jnp.any(match, axis=1).reshape(-1)
    my_ids = lax.dynamic_index_in_dim(tile_lists, me, 0, keepdims=False)
    flat = owners * CAP + rank
    my_slot = lax.dynamic_index_in_dim(flat, me, 0, keepdims=False)
    order = jnp.arange(list_len, dtype=jnp.int32)
    back = jnp.sum(
        (my_slot[None, :] == jnp.arange(slots, dtype=jnp.int32)[:, None]).astype(jnp.int32)
        * order[None, :],
        axis=1,
    )
    hit = (my_ids[None, :] == (labels // TILE)[:, None]).astype(jnp.int32)
    within = labels % TILE
    column = (
        jnp.sum(hit * (order * HALF)[None, :], axis=1)
        + within // HALF * (cols // 2)
        + within % HALF
    )[:, None]
    outgoing = pack_tiles(table.reshape(tiles_here, TILE, width), select)
    chunks = block_rows // 2 // CHUNK
    bf16, f32 = jnp.bfloat16, jnp.float32
    dma = pltpu.SemaphoreType.DMA
    vmem = pl.BlockSpec(memory_space=pltpu.VMEM)
    smem = pl.BlockSpec(memory_space=pltpu.SMEM)
    hbm = pl.BlockSpec(memory_space=pl.ANY)
    grad_emb, returned, loss = pl.pallas_call(
        functools.partial(main_kernel, groups, dp_count, 1.0 / math.sqrt(D)),
        out_shape=(
            jax.ShapeDtypeStruct((block_rows, width), bf16),
            jax.ShapeDtypeStruct((slots, TILE, width), bf16),
            jax.ShapeDtypeStruct((8, 128), f32),
        ),
        in_specs=[smem, smem, hbm, vmem, vmem],
        out_specs=(vmem, hbm, vmem),
        scratch_shapes=[
            pltpu.VMEM((slots, HALF, width), bf16),
            pltpu.VMEM((slots, HALF, width), bf16),
            pltpu.VMEM((cols, width), bf16),
            pltpu.VMEM((block_rows, cols), f32),
            pltpu.VMEM((2, block_rows // 2, cols), f32),
            pltpu.VMEM((block_rows, cols), bf16),
            pltpu.VMEM((list_len, TILE, width), bf16),
            pltpu.VMEM((slots, TILE, width), bf16),
            pltpu.VMEM((CHUNK, 128), f32),
            pltpu.VMEM((8, 128), f32),
            pltpu.VMEM((groups, 8, 128), f32),
            pltpu.VMEM((8, 128), f32),
            pltpu.VMEM((dp_count, 8, 128), f32),
            dma((2, groups)),
            dma((2, groups)),
            dma((2,)),
            dma((2, 2, chunks)),
            dma((2, 2, chunks)),
            dma((2, chunks)),
            dma((2, chunks)),
            dma((2, groups)),
            dma((2, groups)),
            dma,
            dma((groups,)),
            dma((groups,)),
            dma((dp_count,)),
            dma((dp_count,)),
        ],
        compiler_params=pltpu.CompilerParams(
            collective_id=0, has_side_effects=True, vmem_limit_bytes=VMEM_LIMIT
        ),
    )(my_slot, back, outgoing, embeddings, column)
    grad_table, grad_emb = place_tiles(
        returned, jnp.where(taken, select, -1), grad_emb, tiles_here
    )
    return (loss[0, 0] / total_rows, grad_emb, grad_table.reshape(tiles_here * TILE, width))


def fused_bytes(block_rows, width, list_len, groups):
    cols = list_len * TILE
    slots = groups * CAP
    return (
        block_rows * cols * (4 + 4 + 2)
        + 2 * slots * TILE * width * 2
        + 2 * cols * width * 2
        + 2 * block_rows * width * 2
        + block_rows * 128 * 4
    )


def any_body(embeddings, table, tile_lists, labels):
    need = fused_bytes(*embeddings.shape, tile_lists.shape[1], lax.axis_size("proto"))
    if need + 12 * 2**20 <= VMEM_LIMIT:
        return fused_body(embeddings, table, tile_lists, labels)
    return body(embeddings, table, tile_lists, labels)


def solution(mesh):
    placed = (P("proto", "dp"), P("proto", "dp"), P(), P("proto"))
    return jax.shard_map(
        any_body,
        mesh=mesh,
        in_specs=placed,
        out_specs=(P(), P("proto", "dp"), P("proto", "dp")),
        check_vma=False,
    )
```
